32 devices in a mesh: seq: 8 (over z, y), head: 4 (over x, core).
Axes of the slice: x: 2, y: 2, z: 4, core: 2. Of those that a mesh axis runs over, the one named last changes fastest.
Arguments:
- queries: bfloat16 [1024, 32, 128], P('seq', 'head'), may hold values from -6 to 6
- keys: bfloat16 [1024, 2, 128], P('seq'), may hold values from -6 to 6
- values: bfloat16 [1024, 2, 128], P('seq'), may hold values from -6 to 6
- query_map: float32 [32, 128, 128], P('head'), may hold values from -0.5 to 0.5
- key_map: float32 [2, 128, 128], replicated, may hold values from -0.5 to 0.5
- window_logit: float32 [32], P('head'), may hold values from -2 to 2
Outputs:
- student: bfloat16 [1024, 32, 128], P('seq', 'head')
- teacher: bfloat16 [1024, 32, 128], P('seq', 'head')
- query_map_grad: float32 [32, 128, 128], P('head')
- key_map_grad: float32 [2, 128, 128], replicated
- window_grad: float32 [32], P('head')
The draws below stay inside these ranges and needn't reach their ends.
All inputs are finite; a program needn't handle non-finite values.
Results may differ from the reference program's by a relative error of at most 0.0042.
Values may be sent and summed in bfloat16 or wider, within the bound.
A program may use at most 128 MiB of HBM per device.

```python
import jax
import jax.numpy as jnp
from jax import lax

HEAD = 128
GROUP_HEADS = 16
GROUPS = 2
WINDOW = 64
TOK_DEV = 128
HEADS = 32
LENGTH = 1024
N_SEQ = 8


def draw_keys(key, part):
    drawn = jnp.clip(jax.random.normal(jax.random.fold_in(key, 7), (LENGTH, GROUPS, HEAD), jnp.float32), -5.5, 5.5)
    return drawn.astype(jnp.bfloat16)


def draw_queries(key, part):
    drawn = jnp.clip(jax.random.normal(jax.random.fold_in(key, 9), (LENGTH, HEADS, HEAD), jnp.float32), -5.5, 5.5)
    return drawn.astype(jnp.bfloat16)


def block_scale(own_key, extent, shards, low, largest):
    gain = 1.0
    for dim, blocks in shards:
        draws = jax.random.uniform(jax.random.fold_in(jax.random.fold_in(own_key, 6), dim), (blocks,), jnp.float32, low / len(shards), largest / len(shards))
        gain = gain * jnp.repeat(jnp.exp(draws), extent[dim] // blocks).reshape((-1,) + (1,) * (len(extent) - 1 - dim))
    return gain


def bell_draw(rng, extent, scale, bound, split=(), kind=jnp.bfloat16):
    values = jax.random.normal(rng, extent, jnp.float32) * scale
    if len(split) > 0:
        values = block_scale(rng, extent, split, -0.22, 0.18) * values
    return jnp.clip(values, min=-bound, max=bound).astype(kind)


def setup_inputs(seed: int = 0) -> dict:
    streams_of = jax.random.split(jax.random.key(seed), 7)
    queries = draw_queries(jax.random.fold_in(streams_of[6], 71), 0)
    keys = draw_keys(jax.random.fold_in(streams_of[6], 71), 0)
    values = bell_draw(streams_of[2], (LENGTH, GROUPS, HEAD), 1.0, 6.0, ((0, 8),))
    query_map = bell_draw(streams_of[3], (HEADS, HEAD, HEAD), HEAD ** -0.5, 0.5, ((0, 4),), jnp.float32)
    key_map = bell_draw(streams_of[4], (GROUPS, HEAD, HEAD), HEAD ** -0.5, 0.5, (), jnp.float32)
    window_logit = jnp.clip(jax.random.uniform(streams_of[5], (HEADS,), jnp.float32, -2.0, 2.0) * block_scale(streams_of[5], (HEADS,), ((0, 4),), -0.4, 0.0), -2.0, 2.0)
    return dict(queries=queries, keys=keys, values=values, query_map=query_map, key_map=key_map, window_logit=window_logit)


PRECISE = lax.Precision.HIGHEST
NEGATIVE = -1e+30

def hedgehog(preact):
    return jnp.concatenate([jax.nn.softmax(preact, axis=-1), jax.nn.softmax(-preact, axis=-1)], axis=-1)

def teacher_all(queries, keys, values):
    score_scale = HEAD ** (-0.5)
    query_f = queries.astype(jnp.float32).reshape(LENGTH, GROUPS, GROUP_HEADS, HEAD)
    key_f = keys.astype(jnp.float32)
    value_f = values.astype(jnp.float32)
    key_pos = jnp.arange(LENGTH, dtype=jnp.int32)

    def one_block(block_id):
        first_row = (block_id * TOK_DEV).astype(jnp.int32)
        block_q = lax.dynamic_slice_in_dim(query_f, first_row, TOK_DEV, 0)
        scores = jnp.einsum('tgad,kgd->gatk', block_q, key_f, precision=PRECISE) * score_scale
        query_pos = first_row + jnp.arange(TOK_DEV, dtype=jnp.int32)
        allowed = query_pos[:, None] >= key_pos[None, :]
        scores = jnp.where(allowed, scores, NEGATIVE)
        row_peak = lax.optimization_barrier(jnp.max(scores, axis=-1, keepdims=True))
        weights = jnp.where(allowed, jnp.exp(scores - row_peak), 0.0)
        rounded = lax.optimization_barrier(weights.astype(jnp.bfloat16)).astype(jnp.float32)
        mixed = jnp.einsum('gatk,kgd->tgad', rounded, value_f, precision=PRECISE)
        sums = jnp.transpose(lax.optimization_barrier(jnp.sum(weights, axis=-1)), (2, 0, 1))
        return (mixed / sums[..., None]).astype(jnp.bfloat16)
    blocks_out = lax.map(one_block, jnp.arange(N_SEQ, dtype=jnp.int32))
    return blocks_out.reshape(LENGTH, GROUPS * GROUP_HEADS, HEAD)

def student_all(query_map, key_map, window_logit, queries, keys, values):
    blocks = N_SEQ
    block_rows = TOK_DEV
    groups = GROUPS
    group_heads = GROUP_HEADS
    score_scale = HEAD ** (-0.5)
    query_f = queries.astype(jnp.float32).reshape(blocks, block_rows, groups, group_heads, HEAD)
    key_f = keys.astype(jnp.float32)
    value_f = values.astype(jnp.float32)
    key_feats = hedgehog(jnp.einsum('lgd,gde->lge', key_f, key_map, precision=PRECISE))
    feat_width = key_feats.shape[-1]
    block_feats = key_feats.reshape(blocks, block_rows, groups, feat_width)
    block_sums = jnp.einsum('ntgf,ntgd->ngfd', block_feats, value_f.reshape(blocks, block_rows, groups, HEAD), precision=PRECISE)
    block_norms = lax.optimization_barrier(jnp.sum(block_feats, axis=1))
    prior_state = jnp.concatenate([jnp.zeros_like(block_sums[:1]), jnp.cumsum(block_sums, axis=0)[:-1]], axis=0)
    prior_norm = jnp.concatenate([jnp.zeros_like(block_norms[:1]), jnp.cumsum(block_norms, axis=0)[:-1]], axis=0)
    ext_index = (jnp.arange(blocks, dtype=jnp.int32)[:, None] * block_rows + jnp.arange(block_rows + WINDOW, dtype=jnp.int32)[None, :]).astype(jnp.int32)
    key_pad = jnp.concatenate([jnp.zeros((WINDOW, groups, HEAD), jnp.float32), key_f], axis=0)
    value_pad = jnp.concatenate([jnp.zeros((WINDOW, groups, HEAD), jnp.float32), value_f], axis=0)
    feat_pad = jnp.concatenate([jnp.zeros((WINDOW, groups, feat_width), jnp.float32), key_feats], axis=0)
    ext_keys = key_pad[ext_index]
    ext_values = value_pad[ext_index]
    ext_feats = feat_pad[ext_index]
    ext_pos = ext_index - WINDOW
    present = ext_pos >= 0
    query_pos = jnp.arange(blocks, dtype=jnp.int32)[:, None] * block_rows + jnp.arange(block_rows, dtype=jnp.int32)[None, :]
    distance = query_pos[:, :, None] - ext_pos[:, None, :]
    near_mask = (distance >= 0) & (distance < WINDOW) & present[:, None, :]
    far_mask = ((distance >= WINDOW) & present[:, None, :]).astype(jnp.float32)
    rim_feats = ext_feats[:, :WINDOW] * present[:, :WINDOW, None, None].astype(jnp.float32)
    lin_state = prior_state - jnp.einsum('nkgf,nkgd->ngfd', rim_feats, ext_values[:, :WINDOW], precision=PRECISE)
    lin_norm = prior_norm - lax.optimization_barrier(jnp.sum(rim_feats, axis=1))
    scores = jnp.einsum('ntgad,nkgd->ngatk', query_f, ext_keys, precision=PRECISE) * score_scale
    near_full = near_mask[:, None, None, :, :]
    scores = jnp.where(near_full, scores, NEGATIVE)
    window_weights = jnp.where(near_full, jnp.exp(scores - lax.optimization_barrier(jnp.max(scores, axis=-1, keepdims=True))), 0.0)
    query_feats = hedgehog(jnp.einsum('ntgad,gade->ntgae', query_f, query_map.reshape(groups, group_heads, HEAD, HEAD), precision=PRECISE))
    affinity = jnp.einsum('ntgaf,nkgf->ngatk', query_feats, ext_feats, precision=PRECISE) * far_mask[:, None, None, :, :]
    window_mix = jnp.einsum('ngatk,nkgd->ngatd', window_weights, ext_values, precision=PRECISE)
    lin_mix = jnp.einsum('ngatk,nkgd->ngatd', affinity, ext_values, precision=PRECISE) + jnp.einsum('ntgaf,ngfd->ngatd', query_feats, lin_state, precision=PRECISE)
    lin_sum = lax.optimization_barrier(jnp.sum(affinity, axis=-1)) + jnp.einsum('ntgaf,ngf->ngat', query_feats, lin_norm, precision=PRECISE)
    window_share = jax.nn.sigmoid(window_logit).reshape(1, groups, group_heads, 1)
    numerator = window_share[..., None] * window_mix + (1.0 - window_share[..., None]) * lin_mix
    denominator = window_share * lax.optimization_barrier(jnp.sum(window_weights, axis=-1)) + (1.0 - window_share) * lin_sum
    student_f = numerator / denominator[..., None]
    return jnp.transpose(student_f, (0, 3, 1, 2, 4)).reshape(blocks * block_rows, groups * group_heads, HEAD)

def reference(queries, keys, values, query_map, key_map, window_logit):
    teacher = teacher_all(queries, keys, values)
    target = teacher.astype(jnp.float32)

    def objective(query_maps, key_maps, logits):
        student_f = student_all(query_maps, key_maps, logits, queries, keys, values)
        return (0.5 * jnp.sum((student_f - target) ** 2) / LENGTH, student_f)
    gradients, student_f = jax.grad(objective, argnums=(0, 1, 2), has_aux=True)(query_map, key_map, window_logit)
    return (student_f.astype(jnp.bfloat16), teacher, gradients[0], gradients[1], gradients[2])
```

```python
import functools

import jax
import jax.numpy as jnp
from jax import lax
from jax.experimental import pallas as pl
from jax.experimental.pallas import tpu as pltpu
from jax.sharding import PartitionSpec as P

GROUP_HEADS = 16
WINDOW = 64
NEGATIVE = -1e30
F32 = jnp.float32
BF16 = jnp.bfloat16
NN = (((1,), (0,)), ((), ()))
NT = (((1,), (1,)), ((), ()))
TN = (((0,), (0,)), ((), ()))


def mm(a, b, dims):
    return lax.dot_general(a.astype(BF16), b.astype(BF16), dims, preferred_element_type=F32)


def split(x):
    high = x.astype(BF16)
    return high, (x - high.astype(F32)).astype(BF16)


def mm_lhs(x, b, dims):
    high, low = split(x)
    return mm(high, b, dims) + mm(low, b, dims)


def mm_rhs(a, x, dims):
    high, low = split(x)
    return mm(a, high, dims) + mm(a, low, dims)


def soft(x):
    e = jnp.exp(x - jnp.max(x, axis=-1, keepdims=True))
    return e / jnp.sum(e, axis=-1, keepdims=True)


def feature_pull(p, n, dp, dn):
    return p * (dp - jnp.sum(p * dp, axis=-1, keepdims=True)) - n * (
        dn - jnp.sum(n * dn, axis=-1, keepdims=True)
    )


def with_ones(v):
    ones = (lax.broadcasted_iota(jnp.int32, v.shape, 1) == 0).astype(F32).astype(v.dtype)
    return jnp.concatenate([v, ones], axis=1)


def iota(shape, dim):
    return lax.broadcasted_iota(jnp.int32, shape, dim)


def local_kernel(
    sizes, q_ref, kv_ref, mq_ref, mk_ref, logit_ref,
    student_ref, teacher_ref, qgrad_ref, kgrad_ref, lgrad_ref,
    q_scr, out_scr, tea_scr, feat, state, dstate, dext, kpad, vpad, high, low,
):
    count, tok, heads, width, chunk = sizes
    length = count * tok
    scale = width ** (-0.5)
    seq = lax.axis_index("seq")
    first = pl.multiple_of(seq * tok, tok)
    group = lax.axis_index("head") * heads // GROUP_HEADS
    q_scr[...] = q_ref[...].astype(F32).reshape(tok * heads, width)
    kpad[:WINDOW] = jnp.zeros((WINDOW, width), BF16)
    vpad[:WINDOW] = jnp.zeros((WINDOW, width), BF16)
    feat[:WINDOW] = jnp.zeros((WINDOW, 2 * width), F32)
    kpad[WINDOW:] = kv_ref[:, 0].reshape(length, width)
    vpad[WINDOW:] = kv_ref[:, 1].reshape(length, width)
    state[...] = jnp.zeros_like(state)
    dstate[...] = jnp.zeros_like(dstate)
    dext[...] = jnp.zeros_like(dext)
    map_own = mk_ref[group]

    @pl.loop(0, length // chunk)
    def _(c):
        begin = pl.multiple_of(c * chunk, chunk)
        rows = pl.ds(WINDOW + begin, chunk)
        pre = mm_rhs(kpad[rows], map_own, NN)
        kf = jnp.concatenate([soft(pre), soft(-pre)], axis=1)
        feat[rows] = kf
        before = (begin + iota((chunk, 1), 0)) < first - WINDOW
        state[...] += mm(jnp.where(before, kf, 0.0), with_ones(vpad[rows]), TN)

    state_high, state_low = split(state[...])
    high[...] = state_high
    low[...] = state_low
    near = pl.ds(first, tok)
    ext = pl.ds(first, tok + WINDOW)

    @pl.loop(0, heads)
    def _(h):
        mine = pl.ds(h, tok, stride=heads)
        qf32 = q_scr[mine, :]
        q = qf32.astype(BF16)
        scores = mm(q, kpad[WINDOW:], NT) * scale
        seen = first + iota((tok, 1), 0) >= iota((1, length), 1)
        scores = jnp.where(seen, scores, NEGATIVE)
        weights = jnp.exp(scores - jnp.max(scores, axis=-1, keepdims=True))
        total = jnp.sum(weights, axis=-1, keepdims=True)
        teacher = (mm(weights, vpad[WINDOW:], NN) / total).astype(BF16).astype(F32)
        tea_scr[mine, :] = teacher
        sw = mm(q, kpad[ext], NT) * scale
        row, col = iota((tok, tok + WINDOW), 0), iota((tok, tok + WINDOW), 1)
        inside = (col > row) & (col <= row + WINDOW) & (first - WINDOW + col >= 0)
        sw = jnp.where(inside, sw, NEGATIVE)
        ww = jnp.where(inside, jnp.exp(sw - jnp.max(sw, axis=-1, keepdims=True)), 0.0)
        window_sum = jnp.sum(ww, axis=-1, keepdims=True)
        window_mix = mm_lhs(ww, vpad[ext], NN)
        pre = mm_rhs(q, mq_ref[h], NN)
        p, n = soft(pre), soft(-pre)
        qf = jnp.concatenate([p, n], axis=1)
        kf = feat[near].astype(BF16)
        v_near = with_ones(vpad[near])
        far = iota((tok, tok), 0) >= iota((tok, tok), 1)
        aff = jnp.where(far, mm(qf, kf, NT), 0.0)
        lin = mm_lhs(aff, v_near, NN) + mm(qf, high[...], NN) + mm(qf, low[...], NN)
        lin_mix, lin_sum = lin[:, :width], lin[:, width : width + 1]
        share = jax.nn.sigmoid(jnp.full((1, 1), logit_ref[h], F32))
        rest = 1.0 - share
        den = share * window_sum + rest * lin_sum
        out = (share * window_mix + rest * lin_mix) / den
        out_scr[mine, :] = out
        a = (out - teacher) * (1.0 / length) / den
        c = jnp.sum(a * out, axis=-1, keepdims=True)
        dshare = jnp.sum(a * (window_mix - lin_mix), axis=-1, keepdims=True) - c * (
            window_sum - lin_sum
        )
        lgrad_ref[pl.ds(h, 1), :] = jnp.broadcast_to(
            share * rest * jnp.sum(dshare, axis=0, keepdims=True), (1, width)
        )
        first_col = iota((tok, width), 1) == 0
        pull = jnp.concatenate([rest * a, jnp.where(first_col, -rest * c, 0.0)], axis=1)
        daff = jnp.where(far, mm_lhs(pull, v_near, NT), 0.0)
        dqf = mm(daff, kf, NN) + mm(pull, high[...], NT) + mm(pull, low[...], NT)
        dext[...] += mm(daff, qf, TN)
        dstate[...] += mm(qf, pull, TN)
        dpre = feature_pull(p, n, dqf[:, :width], dqf[:, width:])
        qgrad_ref[h] = mm_rhs(q, dpre, TN)

    student_ref[...] = out_scr[...].reshape(tok, heads, width).astype(BF16)
    teacher_ref[...] = tea_scr[...].reshape(tok, heads, width).astype(BF16)

    kgrad_ref[...] = jnp.zeros_like(kgrad_ref)

    @pl.loop(0, length // chunk)
    def _(c):
        begin = pl.multiple_of(c * chunk, chunk)
        rows = pl.ds(WINDOW + begin, chunk)
        before = (begin + iota((chunk, 1), 0)) < first - WINDOW
        dkf = jnp.where(before, mm_rhs(with_ones(vpad[rows]), dstate[...], NT), 0.0)
        kf = feat[rows]
        dpre = feature_pull(kf[:, :width], kf[:, width:], dkf[:, :width], dkf[:, width:])
        kgrad_ref[group] += mm_rhs(kpad[rows], dpre, TN)

    kf, dkf = feat[near], dext[...]
    dpre = feature_pull(kf[:, :width], kf[:, width:], dkf[:, :width], dkf[:, width:])
    kgrad_ref[group] += mm_rhs(kpad[near], dpre, TN)


def shards(queries, keys, values, query_map, key_map, window_logit):
    tok, heads, width = queries.shape
    count = lax.axis_size("seq")
    group = lax.axis_index("head") * heads // GROUP_HEADS
    own = jnp.stack(
        [
            lax.dynamic_index_in_dim(keys, group, 1, keepdims=False),
            lax.dynamic_index_in_dim(values, group, 1, keepdims=False),
        ]
    )
    kv = lax.all_gather(own, "seq", axis=0)
    length = count * tok
    chunk = tok
    while chunk < 1024 and length % (2 * chunk) == 0:
        chunk *= 2
    vm = pl.BlockSpec(memory_space=pltpu.VMEM)
    student, teacher, qgrad, kgrad, lgrad = pl.pallas_call(
        functools.partial(local_kernel, (count, tok, heads, width, chunk)),
        out_shape=(
            jax.ShapeDtypeStruct((tok, heads, width), BF16),
            jax.ShapeDtypeStruct((tok, heads, width), BF16),
            jax.ShapeDtypeStruct((heads, width, width), F32),
            jax.ShapeDtypeStruct(key_map.shape, F32),
            jax.ShapeDtypeStruct((heads, width), F32),
        ),
        in_specs=[vm, vm, vm, vm, pl.BlockSpec(memory_space=pltpu.SMEM)],
        out_specs=(vm,) * 5,
        scratch_shapes=[
            pltpu.VMEM((tok * heads, width), F32),
            pltpu.VMEM((tok * heads, width), F32),
            pltpu.VMEM((tok * heads, width), F32),
            pltpu.VMEM((length + WINDOW, 2 * width), F32),
            pltpu.VMEM((2 * width, 2 * width), F32),
            pltpu.VMEM((2 * width, 2 * width), F32),
            pltpu.VMEM((tok, 2 * width), F32),
            pltpu.VMEM((length + WINDOW, width), BF16),
            pltpu.VMEM((length + WINDOW, width), BF16),
            pltpu.VMEM((2 * width, 2 * width), BF16),
            pltpu.VMEM((2 * width, 2 * width), BF16),
        ],
        compiler_params=pltpu.CompilerParams(vmem_limit_bytes=56 * 2**20),
    )(queries, kv, query_map, key_map, window_logit)
    qgrad, lgrad = lax.psum((qgrad, lgrad), "seq")
    kgrad = lax.psum(kgrad, ("seq", "head"))
    return student, teacher, qgrad, kgrad, lgrad[:, 0]


def solution(mesh):
    placed = (
        P("seq", "head", None),
        P("seq", None, None),
        P("seq", None, None),
        P("head", None, None),
        P(),
        P("head"),
    )
    return jax.shard_map(
        shards,
        mesh=mesh,
        in_specs=placed,
        out_specs=(
            P("seq", "head", None),
            P("seq", "head", None),
            P("head", None, None),
            P(),
            P("head"),
        ),
        check_vma=False,
    )
```

```python
import functools

import jax
import jax.numpy as jnp
from jax import lax
from jax.experimental import pallas as pl
from jax.experimental.pallas import tpu as pltpu
from jax.sharding import PartitionSpec as P

GROUP_HEADS = 16
WINDOW = 64
NEGATIVE = -1e30
F32 = jnp.float32
BF16 = jnp.bfloat16
NN = (((1,), (0,)), ((), ()))
NT = (((1,), (1,)), ((), ()))
TN = (((0,), (0,)), ((), ()))


def mm(a, b, dims):
    return lax.dot_general(a.astype(BF16), b.astype(BF16), dims, preferred_element_type=F32)


def split(x):
    high = x.astype(BF16)
    return high, (x - high.astype(F32)).astype(BF16)


def mm_lhs(x, b, dims):
    high, low = split(x)
    return mm(high, b, dims) + mm(low, b, dims)


def mm_rhs(a, x, dims):
    high, low = split(x)
    return mm(a, high, dims) + mm(a, low, dims)


def soft(x):
    e = jnp.exp(x - jnp.max(x, axis=-1, keepdims=True))
    return e / jnp.sum(e, axis=-1, keepdims=True)


def feature_pull(p, n, dp, dn):
    return p * (dp - jnp.sum(p * dp, axis=-1, keepdims=True)) - n * (
        dn - jnp.sum(n * dn, axis=-1, keepdims=True)
    )


def with_ones(v):
    ones = (lax.broadcasted_iota(jnp.int32, v.shape, 1) == 0).astype(F32).astype(v.dtype)
    return jnp.concatenate([v, ones], axis=1)


def iota(shape, dim):
    return lax.broadcasted_iota(jnp.int32, shape, dim)


def local_kernel(
    sizes, q_ref, kv_ref, mq_ref, mk_ref, logit_ref,
    student_ref, teacher_ref, qgrad_ref, kgrad_ref, lgrad_ref,
    q_scr, out_scr, tea_scr, feat, state, dstate, dext, kpad, vpad, high, low,
):
    count, tok, heads, width, chunk = sizes
    length = count * tok
    scale = width ** (-0.5)
    seq = lax.axis_index("seq")
    first = pl.multiple_of(seq * tok, tok)
    group = lax.axis_index("head") * heads // GROUP_HEADS
    q_scr[...] = q_ref[...].astype(F32).reshape(tok * heads, width)
    kpad[:WINDOW] = jnp.zeros((WINDOW, width), BF16)
    vpad[:WINDOW] = jnp.zeros((WINDOW, width), BF16)
    feat[:WINDOW] = jnp.zeros((WINDOW, 2 * width), F32)
    kpad[WINDOW:] = kv_ref[:, 0].reshape(length, width)
    vpad[WINDOW:] = kv_ref[:, 1].reshape(length, width)
    state[...] = jnp.zeros_like(state)
    dstate[...] = jnp.zeros_like(dstate)
    dext[...] = jnp.zeros_like(dext)
    map_own = mk_ref[group]

    @pl.loop(0, length // chunk)
    def _(c):
        begin = pl.multiple_of(c * chunk, chunk)
        rows = pl.ds(WINDOW + begin, chunk)
        pre = mm_rhs(kpad[rows], map_own, NN)
        kf = jnp.concatenate([soft(pre), soft(-pre)], axis=1)
        feat[rows] = kf
        before = (begin + iota((chunk, 1), 0)) < first - WINDOW
        state[...] += mm(jnp.where(before, kf, 0.0), with_ones(vpad[rows]), TN)

    state_high, state_low = split(state[...])
    high[...] = state_high
    low[...] = state_low
    near = pl.ds(first, tok)
    ext = pl.ds(first, tok + WINDOW)

    @pl.loop(0, heads)
    def _(h):
        mine = pl.ds(h, tok, stride=heads)
        qf32 = q_scr[mine, :]
        q = qf32.astype(BF16)
        scores = mm(q, kpad[WINDOW:], NT) * scale
        seen = first + iota((tok, 1), 0) >= iota((1, length), 1)
        scores = jnp.where(seen, scores, NEGATIVE)
        weights = jnp.exp(scores - jnp.max(scores, axis=-1, keepdims=True))
        total = jnp.sum(weights, axis=-1, keepdims=True)
        teacher = (mm(weights, vpad[WINDOW:], NN) / total).astype(BF16).astype(F32)
        tea_scr[mine, :] = teacher
        sw = mm(q, kpad[ext], NT) * scale
        row, col = iota((tok, tok + WINDOW), 0), iota((tok, tok + WINDOW), 1)
        inside = (col > row) & (col <= row + WINDOW) & (first - WINDOW + col >= 0)
        sw = jnp.where(inside, sw, NEGATIVE)
        ww = jnp.where(inside, jnp.exp(sw - jnp.max(sw, axis=-1, keepdims=True)), 0.0)
        window_sum = jnp.sum(ww, axis=-1, keepdims=True)
        window_mix = mm_lhs(ww, vpad[ext], NN)
        pre = mm_rhs(q, mq_ref[h], NN)
        p, n = soft(pre), soft(-pre)
        qf = jnp.concatenate([p, n], axis=1)
        kf = feat[near].astype(BF16)
        v_near = with_ones(vpad[near])
        far = iota((tok, tok), 0) >= iota((tok, tok), 1)
        aff = jnp.where(far, mm(qf, kf, NT), 0.0)
        lin = mm_lhs(aff, v_near, NN) + mm(qf, high[...], NN) + mm(qf, low[...], NN)
        lin_mix, lin_sum = lin[:, :width], lin[:, width : width + 1]
        share = jax.nn.sigmoid(jnp.full((1, 1), logit_ref[h], F32))
        rest = 1.0 - share
        den = share * window_sum + rest * lin_sum
        out = (share * window_mix + rest * lin_mix) / den
        out_scr[mine, :] = out
        a = (out - teacher) * (1.0 / length) / den
        c = jnp.sum(a * out, axis=-1, keepdims=True)
        dshare = jnp.sum(a * (window_mix - lin_mix), axis=-1, keepdims=True) - c * (
            window_sum - lin_sum
        )
        lgrad_ref[pl.ds(h, 1), :] = jnp.broadcast_to(
            share * rest * jnp.sum(dshare, axis=0, keepdims=True), (1, width)
        )
        first_col = iota((tok, width), 1) == 0
        pull = jnp.concatenate([rest * a, jnp.where(first_col, -rest * c, 0.0)], axis=1)
        daff = jnp.where(far, mm_lhs(pull, v_near, NT), 0.0)
        dqf = mm(daff, kf, NN) + mm(pull, high[...], NT) + mm(pull, low[...], NT)
        dext[...] += mm(daff, qf, TN)
        dstate[...] += mm(qf, pull, TN)
        dpre = feature_pull(p, n, dqf[:, :width], dqf[:, width:])
        qgrad_ref[h] = mm_rhs(q, dpre, TN)

    student_ref[...] = out_scr[...].reshape(tok, heads, width).astype(BF16)
    teacher_ref[...] = tea_scr[...].reshape(tok, heads, width).astype(BF16)

    kgrad_ref[...] = jnp.zeros_like(kgrad_ref)

    @pl.loop(0, length // chunk)
    def _(c):
        begin = pl.multiple_of(c * chunk, chunk)
        rows = pl.ds(WINDOW + begin, chunk)
        before = (begin + iota((chunk, 1), 0)) < first - WINDOW
        dkf = jnp.where(before, mm_rhs(with_ones(vpad[rows]), dstate[...], NT), 0.0)
        kf = feat[rows]
        dpre = feature_pull(kf[:, :width], kf[:, width:], dkf[:, :width], dkf[:, width:])
        kgrad_ref[...] += mm_rhs(kpad[rows], dpre, TN)

    kf, dkf = feat[near], dext[...]
    dpre = feature_pull(kf[:, :width], kf[:, width:], dkf[:, :width], dkf[:, width:])
    kgrad_ref[...] += mm_rhs(kpad[near], dpre, TN)


def meet(axes):
    barrier = pltpu.get_barrier_semaphore()
    signals = 0
    for axis in axes:
        count = lax.axis_size(axis)
        me = lax.axis_index(axis)
        for k in range(1, count):
            pl.semaphore_signal(
                barrier, inc=1, device_id={axis: lax.rem(me + k, count)},
                device_id_type=pl.DeviceIdType.MESH,
            )
            signals += 1
    pl.semaphore_wait(barrier, signals)


def push(axis, source, slots, send_sem, recv_sem):
    count = lax.axis_size(axis)
    me = lax.axis_index(axis)
    copies = []
    for k in range(1, count):
        peer = lax.rem(me + k, count)
        copy = pltpu.make_async_remote_copy(
            src_ref=source(peer),
            dst_ref=slots.at[k - 1],
            send_sem=send_sem.at[k - 1],
            recv_sem=recv_sem.at[k - 1],
            device_id={axis: peer},
            device_id_type=pl.DeviceIdType.MESH,
        )
        copy.start()
        copies.append(copy)
    return copies


def gather_kernel(own_ref, kv_ref, slots, send_sem, recv_sem):
    count = lax.axis_size("seq")
    me = lax.axis_index("seq")
    meet(("seq",))
    copies = push("seq", lambda peer: own_ref, slots, send_sem, recv_sem)
    kv_ref[me] = own_ref[...]
    for k, copy in enumerate(copies, 1):
        copy.wait_recv()
        kv_ref[lax.rem(me + count - k, count)] = slots[k - 1]
    for copy in copies:
        copy.wait_send()


def reduce_kernel(
    sizes, q_ref, k_ref, l_ref, qsum_ref, ksum_ref, lsum_ref,
    pieces, landed, total, parts, own_k, other_k, send1, recv1, send2, recv2, send3, recv3,
):
    heads, groups = sizes
    count, ranks = lax.axis_size("seq"), lax.axis_size("head")
    me, rank = lax.axis_index("seq"), lax.axis_index("head")
    q_rows, k_rows, l_rows = q_ref.shape[1], k_ref.shape[1], l_ref.shape[0]
    q_part = pl.ds(0, q_rows)
    l_part = pl.ds(q_rows, l_rows)
    k_part = pl.ds(q_rows + l_rows, k_rows)
    pieces[:, q_part] = q_ref[...]
    pieces[:, k_part] = k_ref[...]
    for piece in range(count):
        pieces[piece, l_part] = l_ref[...]
    meet(("seq", "head"))
    first = push("seq", lambda peer: pieces.at[peer], landed, send1, recv1)
    summed = pieces[me]
    for k, copy in enumerate(first):
        copy.wait_recv()
        summed = summed + landed[k]
    total[...] = summed
    second = push("seq", lambda peer: total, parts, send2, recv2)
    qsum_ref[me] = total[q_part]
    own_k[me] = total[k_part]
    lsum_ref[...] = total[l_part]
    for k, copy in enumerate(second, 1):
        copy.wait_recv()
        origin = lax.rem(me + count - k, count)
        qsum_ref[origin] = parts[k - 1, q_part]
        own_k[origin] = parts[k - 1, k_part]
    third = push("head", lambda peer: own_k, other_k, send3, recv3)
    ksum_ref[...] = jnp.zeros_like(ksum_ref)
    ksum_ref[rank * heads // GROUP_HEADS] = own_k[...]
    for k, copy in enumerate(third, 1):
        copy.wait_recv()
        origin = lax.rem(rank + ranks - k, ranks)
        ksum_ref[origin * heads // GROUP_HEADS] += other_k[k - 1]
    for copy in first + second + third:
        copy.wait_send()


def shards(queries, keys, values, query_map, key_map, window_logit):
    tok, heads, width = queries.shape
    count = lax.axis_size("seq")
    group = lax.axis_index("head") * heads // GROUP_HEADS
    own = jnp.stack(
        [
            lax.dynamic_index_in_dim(keys, group, 1, keepdims=False),
            lax.dynamic_index_in_dim(values, group, 1, keepdims=False),
        ]
    )
    vm = pl.BlockSpec(memory_space=pltpu.VMEM)
    dma = pltpu.SemaphoreType.DMA
    kv = pl.pallas_call(
        gather_kernel,
        out_shape=jax.ShapeDtypeStruct((count,) + own.shape, BF16),
        in_specs=[vm],
        out_specs=vm,
        scratch_shapes=[
            pltpu.VMEM((count - 1,) + own.shape, BF16),
            dma((count - 1,)),
            dma((count - 1,)),
        ],
        compiler_params=pltpu.CompilerParams(
            collective_id=0, has_side_effects=True, vmem_limit_bytes=40 * 2**20
        ),
    )(own)
    length = count * tok
    chunk = tok
    while chunk < 1024 and length % (2 * chunk) == 0:
        chunk *= 2
    student, teacher, qgrad, kgrad, lgrad = pl.pallas_call(
        functools.partial(local_kernel, (count, tok, heads, width, chunk)),
        out_shape=(
            jax.ShapeDtypeStruct((tok, heads, width), BF16),
            jax.ShapeDtypeStruct((tok, heads, width), BF16),
            jax.ShapeDtypeStruct((heads, width, width), F32),
            jax.ShapeDtypeStruct((width, width), F32),
            jax.ShapeDtypeStruct((heads, width), F32),
        ),
        in_specs=[vm, vm, vm, vm, pl.BlockSpec(memory_space=pltpu.SMEM)],
        out_specs=(vm,) * 5,
        scratch_shapes=[
            pltpu.VMEM((tok * heads, width), F32),
            pltpu.VMEM((tok * heads, width), F32),
            pltpu.VMEM((tok * heads, width), F32),
            pltpu.VMEM((length + WINDOW, 2 * width), F32),
            pltpu.VMEM((2 * width, 2 * width), F32),
            pltpu.VMEM((2 * width, 2 * width), F32),
            pltpu.VMEM((tok, 2 * width), F32),
            pltpu.VMEM((length + WINDOW, width), BF16),
            pltpu.VMEM((length + WINDOW, width), BF16),
            pltpu.VMEM((2 * width, 2 * width), BF16),
            pltpu.VMEM((2 * width, 2 * width), BF16),
        ],
        compiler_params=pltpu.CompilerParams(vmem_limit_bytes=56 * 2**20),
    )(queries, kv, query_map, key_map, window_logit)
    ranks, groups = lax.axis_size("head"), key_map.shape[0]
    q_rows, k_rows = heads * width // count, width // count
    rows = q_rows + heads + k_rows
    qgrad, kgrad, lgrad = pl.pallas_call(
        functools.partial(reduce_kernel, (heads, groups)),
        out_shape=(
            jax.ShapeDtypeStruct((count, q_rows, width), F32),
            jax.ShapeDtypeStruct((groups, count, k_rows, width), F32),
            jax.ShapeDtypeStruct((heads, width), F32),
        ),
        in_specs=[vm] * 3,
        out_specs=(vm,) * 3,
        scratch_shapes=[
            pltpu.VMEM((count, rows, width), F32),
            pltpu.VMEM((count - 1, rows, width), F32),
            pltpu.VMEM((rows, width), F32),
            pltpu.VMEM((count - 1, rows, width), F32),
            pltpu.VMEM((count, k_rows, width), F32),
            pltpu.VMEM((ranks - 1, count, k_rows, width), F32),
            dma((count - 1,)),
            dma((count - 1,)),
            dma((count - 1,)),
            dma((count - 1,)),
            dma((ranks - 1,)),
            dma((ranks - 1,)),
        ],
        compiler_params=pltpu.CompilerParams(
            collective_id=1, has_side_effects=True, vmem_limit_bytes=40 * 2**20
        ),
    )(
        qgrad.reshape(count, q_rows, width),
        kgrad.reshape(count, k_rows, width),
        lgrad,
    )
    qgrad = qgrad.reshape(query_map.shape)
    kgrad = kgrad.reshape(key_map.shape)
    return student, teacher, qgrad, kgrad, lgrad[:, 0]


def solution(mesh):
    placed = (
        P("seq", "head", None),
        P("seq", None, None),
        P("seq", None, None),
        P("head", None, None),
        P(),
        P("head"),
    )
    return jax.shard_map(
        shards,
        mesh=mesh,
        in_specs=placed,
        out_specs=(
            P("seq", "head", None),
            P("seq", "head", None),
            P("head", None, None),
            P(),
            P("head"),
        ),
        check_vma=False,
    )
```

```python
import functools

import jax
import jax.numpy as jnp
from jax import lax
from jax.experimental import pallas as pl
from jax.experimental.pallas import tpu as pltpu
from jax.sharding import PartitionSpec as P

GROUP_HEADS = 16
WINDOW = 64
NEGATIVE = -1e30
F32 = jnp.float32
BF16 = jnp.bfloat16
NN = (((1,), (0,)), ((), ()))
NT = (((1,), (1,)), ((), ()))
TN = (((0,), (0,)), ((), ()))


def mm(a, b, dims):
    return lax.dot_general(a.astype(BF16), b.astype(BF16), dims, preferred_element_type=F32)


def split(x):
    high = x.astype(BF16)
    return high, (x - high.astype(F32)).astype(BF16)


def mm_lhs(x, b, dims):
    high, low = split(x)
    return mm(high, b, dims) + mm(low, b, dims)


def mm_rhs(a, x, dims):
    high, low = split(x)
    return mm(a, high, dims) + mm(a, low, dims)


def soft(x):
    e = jnp.exp(x - jnp.max(x, axis=-1, keepdims=True))
    return e / jnp.sum(e, axis=-1, keepdims=True)


def feature_pull(p, n, dp, dn):
    return p * (dp - jnp.sum(p * dp, axis=-1, keepdims=True)) - n * (
        dn - jnp.sum(n * dn, axis=-1, keepdims=True)
    )


def with_ones(v):
    ones = (lax.broadcasted_iota(jnp.int32, v.shape, 1) == 0).astype(F32).astype(v.dtype)
    return jnp.concatenate([v, ones], axis=1)


def iota(shape, dim):
    return lax.broadcasted_iota(jnp.int32, shape, dim)


def local_kernel(
    sizes, q_ref, kv_ref, mq_ref, mk_ref, logit_ref,
    student_ref, teacher_ref, qgrad_ref, kgrad_ref, lgrad_ref,
    q_scr, out_scr, tea_scr, feat, state, dstate, dext, kpad, vpad, high, low,
):
    count, tok, heads, width, chunk = sizes
    length = count * tok
    scale = width ** (-0.5)
    seq = lax.axis_index("seq")
    first = pl.multiple_of(seq * tok, tok)
    group = lax.axis_index("head") * heads // GROUP_HEADS
    q_scr[...] = q_ref[...].astype(F32).reshape(tok * heads, width)
    kpad[:WINDOW] = jnp.zeros((WINDOW, width), BF16)
    vpad[:WINDOW] = jnp.zeros((WINDOW, width), BF16)
    feat[:WINDOW] = jnp.zeros((WINDOW, 2 * width), F32)
    kpad[WINDOW:] = kv_ref[:, 0].reshape(length, width)
    vpad[WINDOW:] = kv_ref[:, 1].reshape(length, width)
    state[...] = jnp.zeros_like(state)
    dstate[...] = jnp.zeros_like(dstate)
    dext[...] = jnp.zeros_like(dext)
    map_own = mk_ref[group]

    @pl.loop(0, length // chunk)
    def _(c):
        begin = pl.multiple_of(c * chunk, chunk)
        rows = pl.ds(WINDOW + begin, chunk)
        pre = mm_rhs(kpad[rows], map_own, NN)
        kf = jnp.concatenate([soft(pre), soft(-pre)], axis=1)
        feat[rows] = kf
        before = (begin + iota((chunk, 1), 0)) < first - WINDOW
        state[...] += mm(jnp.where(before, kf, 0.0), with_ones(vpad[rows]), TN)

    state_high, state_low = split(state[...])
    high[...] = state_high
    low[...] = state_low
    near = pl.ds(first, tok)
    ext = pl.ds(first, tok + WINDOW)

    @pl.loop(0, heads)
    def _(h):
        mine = pl.ds(h, tok, stride=heads)
        qf32 = q_scr[mine, :]
        q = qf32.astype(BF16)
        scores = mm(q, kpad[WINDOW:], NT) * scale
        seen = first + iota((tok, 1), 0) >= iota((1, length), 1)
        scores = jnp.where(seen, scores, NEGATIVE)
        weights = jnp.exp(scores - jnp.max(scores, axis=-1, keepdims=True))
        total = jnp.sum(weights, axis=-1, keepdims=True)
        teacher = (mm(weights, vpad[WINDOW:], NN) / total).astype(BF16).astype(F32)
        tea_scr[mine, :] = teacher
        sw = mm(q, kpad[ext], NT) * scale
        row, col = iota((tok, tok + WINDOW), 0), iota((tok, tok + WINDOW), 1)
        inside = (col > row) & (col <= row + WINDOW) & (first - WINDOW + col >= 0)
        sw = jnp.where(inside, sw, NEGATIVE)
        ww = jnp.where(inside, jnp.exp(sw - jnp.max(sw, axis=-1, keepdims=True)), 0.0)
        window_sum = jnp.sum(ww, axis=-1, keepdims=True)
        window_mix = mm_lhs(ww, vpad[ext], NN)
        pre = mm_rhs(q, mq_ref[h], NN)
        p, n = soft(pre), soft(-pre)
        qf = jnp.concatenate([p, n], axis=1)
        kf = feat[near].astype(BF16)
        v_near = with_ones(vpad[near])
        far = iota((tok, tok), 0) >= iota((tok, tok), 1)
        aff = jnp.where(far, mm(qf, kf, NT), 0.0)
        lin = mm_lhs(aff, v_near, NN) + mm(qf, high[...], NN) + mm(qf, low[...], NN)
        lin_mix, lin_sum = lin[:, :width], lin[:, width : width + 1]
        share = jax.nn.sigmoid(jnp.full((1, 1), logit_ref[h], F32))
        rest = 1.0 - share
        den = share * window_sum + rest * lin_sum
        out = (share * window_mix + rest * lin_mix) / den
        out_scr[mine, :] = out
        a = (out - teacher) * (1.0 / length) / den
        c = jnp.sum(a * out, axis=-1, keepdims=True)
        dshare = jnp.sum(a * (window_mix - lin_mix), axis=-1, keepdims=True) - c * (
            window_sum - lin_sum
        )
        lgrad_ref[pl.ds(h, 1), :] = jnp.broadcast_to(
            share * rest * jnp.sum(dshare, axis=0, keepdims=True), (1, width)
        )
        first_col = iota((tok, width), 1) == 0
        pull = jnp.concatenate([rest * a, jnp.where(first_col, -rest * c, 0.0)], axis=1)
        daff = jnp.where(far, mm_lhs(pull, v_near, NT), 0.0)
        dqf = mm(daff, kf, NN) + mm(pull, high[...], NT) + mm(pull, low[...], NT)
        dext[...] += mm(daff, qf, TN)
        dstate[...] += mm(qf, pull, TN)
        dpre = feature_pull(p, n, dqf[:, :width], dqf[:, width:])
        qgrad_ref[h] = mm_rhs(q, dpre, TN)

    student_ref[...] = out_scr[...].reshape(tok, heads, width).astype(BF16)
    teacher_ref[...] = tea_scr[...].reshape(tok, heads, width).astype(BF16)

    kgrad_ref[...] = jnp.zeros_like(kgrad_ref)

    @pl.loop(0, length // chunk)
    def _(c):
        begin = pl.multiple_of(c * chunk, chunk)
        rows = pl.ds(WINDOW + begin, chunk)
        before = (begin + iota((chunk, 1), 0)) < first - WINDOW
        dkf = jnp.where(before, mm_rhs(with_ones(vpad[rows]), dstate[...], NT), 0.0)
        kf = feat[rows]
        dpre = feature_pull(kf[:, :width], kf[:, width:], dkf[:, :width], dkf[:, width:])
        kgrad_ref[...] += mm_rhs(kpad[rows], dpre, TN)

    kf, dkf = feat[near], dext[...]
    dpre = feature_pull(kf[:, :width], kf[:, width:], dkf[:, :width], dkf[:, width:])
    kgrad_ref[...] += mm_rhs(kpad[near], dpre, TN)


def meet(axes):
    barrier = pltpu.get_barrier_semaphore()
    signals = 0
    for axis in axes:
        count = lax.axis_size(axis)
        me = lax.axis_index(axis)
        for k in range(1, count):
            pl.semaphore_signal(
                barrier, inc=1, device_id={axis: lax.rem(me + k, count)},
                device_id_type=pl.DeviceIdType.MESH,
            )
            signals += 1
    pl.semaphore_wait(barrier, signals)


def push(axis, source, slots, send_sem, recv_sem):
    count = lax.axis_size(axis)
    me = lax.axis_index(axis)
    copies = []
    for k in range(1, count):
        peer = lax.rem(me + k, count)
        copy = pltpu.make_async_remote_copy(
            src_ref=source(peer),
            dst_ref=slots.at[k - 1],
            send_sem=send_sem.at[k - 1],
            recv_sem=recv_sem.at[k - 1],
            device_id={axis: peer},
            device_id_type=pl.DeviceIdType.MESH,
        )
        copy.start()
        copies.append(copy)
    return copies


def gather_kernel(own_ref, kv_ref, slots, send_sem, recv_sem):
    count = lax.axis_size("seq")
    me = lax.axis_index("seq")
    meet(("seq",))
    copies = push("seq", lambda peer: own_ref, slots, send_sem, recv_sem)
    kv_ref[me] = own_ref[...]
    for k, copy in enumerate(copies, 1):
        copy.wait_recv()
        kv_ref[lax.rem(me + count - k, count)] = slots[k - 1]
    for copy in copies:
        copy.wait_send()


def reduce_kernel(
    sizes, q_ref, k_ref, l_ref, qsum_ref, ksum_ref, lsum_ref,
    pieces, landed, total, parts, own_k, other_k, send1, recv1, send2, recv2, send3, recv3,
):
    heads, groups = sizes
    count, ranks = lax.axis_size("seq"), lax.axis_size("head")
    me, rank = lax.axis_index("seq"), lax.axis_index("head")
    q_rows, k_rows, l_rows = q_ref.shape[1], k_ref.shape[1], l_ref.shape[0]
    q_part = pl.ds(0, q_rows)
    k_part = pl.ds(q_rows + 2 * l_rows, k_rows)

    def logits_of(block):
        return block[q_rows : q_rows + l_rows] + block[q_rows + l_rows : q_rows + 2 * l_rows]

    pieces[...] = jnp.zeros_like(pieces)
    pieces[:, q_part] = q_ref[...].astype(BF16)
    pieces[:, k_part] = k_ref[...].astype(BF16)
    l_both = jnp.concatenate(split(l_ref[...]), axis=0)
    for piece in range(count):
        pieces[piece, pl.ds(q_rows, 2 * l_rows)] = l_both
    meet(("seq", "head"))
    first = push("seq", lambda peer: pieces.at[peer], landed, send1, recv1)
    q_sum, k_sum = q_ref[me], k_ref[me]
    l_sum = logits_of(pieces[me].astype(F32))
    for k, copy in enumerate(first):
        copy.wait_recv()
        block = landed[k].astype(F32)
        q_sum = q_sum + block[:q_rows]
        l_sum = l_sum + logits_of(block)
        k_sum = k_sum + block[q_rows + 2 * l_rows : q_rows + 2 * l_rows + k_rows]
    total[...] = jnp.zeros_like(total)
    total[q_part] = q_sum.astype(BF16)
    total[k_part] = k_sum.astype(BF16)
    total[pl.ds(q_rows, 2 * l_rows)] = jnp.concatenate(split(l_sum), axis=0)
    second = push("seq", lambda peer: total, parts, send2, recv2)
    qsum_ref[me] = total[q_part].astype(F32)
    own_k[me] = total[k_part].astype(F32)
    mine = logits_of(total[...].astype(F32))
    lsum_ref[...] = jnp.where(me == 0, mine, 0.0)
    for k, copy in enumerate(second, 1):
        copy.wait_recv()
        origin = lax.rem(me + count - k, count)
        block = parts[k - 1].astype(F32)
        qsum_ref[origin] = block[:q_rows]
        own_k[origin] = block[q_rows + 2 * l_rows : q_rows + 2 * l_rows + k_rows]
        lsum_ref[...] += jnp.where(origin == 0, logits_of(block), 0.0)
    third = push("head", lambda peer: own_k, other_k, send3, recv3)
    ksum_ref[...] = jnp.zeros_like(ksum_ref)
    ksum_ref[rank * heads // GROUP_HEADS] = own_k[...]
    for k, copy in enumerate(third, 1):
        copy.wait_recv()
        origin = lax.rem(rank + ranks - k, ranks)
        ksum_ref[origin * heads // GROUP_HEADS] += other_k[k - 1]
    for copy in first + second + third:
        copy.wait_send()


def shards(queries, keys, values, query_map, key_map, window_logit):
    tok, heads, width = queries.shape
    count = lax.axis_size("seq")
    group = lax.axis_index("head") * heads // GROUP_HEADS
    own = jnp.stack(
        [
            lax.dynamic_index_in_dim(keys, group, 1, keepdims=False),
            lax.dynamic_index_in_dim(values, group, 1, keepdims=False),
        ]
    )
    vm = pl.BlockSpec(memory_space=pltpu.VMEM)
    dma = pltpu.SemaphoreType.DMA
    kv = pl.pallas_call(
        gather_kernel,
        out_shape=jax.ShapeDtypeStruct((count,) + own.shape, BF16),
        in_specs=[vm],
        out_specs=vm,
        scratch_shapes=[
            pltpu.VMEM((count - 1,) + own.shape, BF16),
            dma((count - 1,)),
            dma((count - 1,)),
        ],
        compiler_params=pltpu.CompilerParams(
            collective_id=0, has_side_effects=True, vmem_limit_bytes=40 * 2**20
        ),
    )(own)
    length = count * tok
    chunk = tok
    while chunk < 1024 and length % (2 * chunk) == 0:
        chunk *= 2
    student, teacher, qgrad, kgrad, lgrad = pl.pallas_call(
        functools.partial(local_kernel, (count, tok, heads, width, chunk)),
        out_shape=(
            jax.ShapeDtypeStruct((tok, heads, width), BF16),
            jax.ShapeDtypeStruct((tok, heads, width), BF16),
            jax.ShapeDtypeStruct((heads, width, width), F32),
            jax.ShapeDtypeStruct((width, width), F32),
            jax.ShapeDtypeStruct((heads, width), F32),
        ),
        in_specs=[vm, vm, vm, vm, pl.BlockSpec(memory_space=pltpu.SMEM)],
        out_specs=(vm,) * 5,
        scratch_shapes=[
            pltpu.VMEM((tok * heads, width), F32),
            pltpu.VMEM((tok * heads, width), F32),
            pltpu.VMEM((tok * heads, width), F32),
            pltpu.VMEM((length + WINDOW, 2 * width), F32),
            pltpu.VMEM((2 * width, 2 * width), F32),
            pltpu.VMEM((2 * width, 2 * width), F32),
            pltpu.VMEM((tok, 2 * width), F32),
            pltpu.VMEM((length + WINDOW, width), BF16),
            pltpu.VMEM((length + WINDOW, width), BF16),
            pltpu.VMEM((2 * width, 2 * width), BF16),
            pltpu.VMEM((2 * width, 2 * width), BF16),
        ],
        compiler_params=pltpu.CompilerParams(vmem_limit_bytes=56 * 2**20),
    )(queries, kv, query_map, key_map, window_logit)
    ranks, groups = lax.axis_size("head"), key_map.shape[0]
    q_rows, k_rows = heads * width // count, width // count
    rows = -(-(q_rows + 2 * heads + k_rows) // 16) * 16
    qgrad, kgrad, lgrad = pl.pallas_call(
        functools.partial(reduce_kernel, (heads, groups)),
        out_shape=(
            jax.ShapeDtypeStruct((count, q_rows, width), F32),
            jax.ShapeDtypeStruct((groups, count, k_rows, width), F32),
            jax.ShapeDtypeStruct((heads, width), F32),
        ),
        in_specs=[vm] * 3,
        out_specs=(vm,) * 3,
        scratch_shapes=[
            pltpu.VMEM((count, rows, width), BF16),
            pltpu.VMEM((count - 1, rows, width), BF16),
            pltpu.VMEM((rows, width), BF16),
            pltpu.VMEM((count - 1, rows, width), BF16),
            pltpu.VMEM((count, k_rows, width), F32),
            pltpu.VMEM((ranks - 1, count, k_rows, width), F32),
            dma((count - 1,)),
            dma((count - 1,)),
            dma((count - 1,)),
            dma((count - 1,)),
            dma((ranks - 1,)),
            dma((ranks - 1,)),
        ],
        compiler_params=pltpu.CompilerParams(
            collective_id=1, has_side_effects=True, vmem_limit_bytes=40 * 2**20
        ),
    )(
        qgrad.reshape(count, q_rows, width),
        kgrad.reshape(count, k_rows, width),
        lgrad,
    )
    qgrad = qgrad.reshape(query_map.shape)
    kgrad = kgrad.reshape(key_map.shape)
    return student, teacher, qgrad, kgrad, lgrad[:, 0]


def solution(mesh):
    placed = (
        P("seq", "head", None),
        P("seq", None, None),
        P("seq", None, None),
        P("head", None, None),
        P(),
        P("head"),
    )
    return jax.shard_map(
        shards,
        mesh=mesh,
        in_specs=placed,
        out_specs=(
            P("seq", "head", None),
            P("seq", "head", None),
            P("head", None, None),
            P(),
            P("head"),
        ),
        check_vma=False,
    )
```
